256 devices in a mesh: angle: 16 (over y, x), panel: 16 (over z, core).
Axes of the slice: x: 4, y: 4, z: 8, core: 2. Of those that a mesh axis runs over, the one named last changes fastest.
Arguments:
- measured: bfloat16 [512, 512, 1024], P(('angle', 'panel')), may hold values from 0.099609375 to 1
- predicted: bfloat16 [512, 512, 1024], P(('angle', 'panel')), may hold values from 0 to 2
- slice_filter: bfloat16 [512, 512], replicated, may hold values from -0.25 to 0.25
- column_filter: bfloat16 [1024, 1024], replicated, may hold values from -0.1875 to 0.1875
- volume: float32 [512, 32768], P('angle', 'panel'), may hold values from 0 to 1
- tiles: bfloat16 [3072, 128, 128], P('panel'), may hold values from -0.5 to 0.5
- tile_ray: int32 [3072], P('panel'), may hold values from 0 to 255
- tile_vox: int32 [3072], P('panel'), may hold values from 0 to 255
- live_tiles: int32 [16], P('panel'), may hold values from 1 to 192, as said below
Outputs:
- updated_volume: float32 [512, 32768], P('angle', 'panel')
- projected: bfloat16 [512, 512, 1024], P(('angle', 'panel'))
The draws below stay inside these ranges and needn't reach their ends.
Inputs may be any that keep to these rules, and one draw needn't show every extreme that they name: live_tiles[p] counts the tile slots of panel p that are used, from the first slot on; at least one panel uses all 192 slots.
All inputs are finite; a program needn't handle non-finite values.
Results may differ from the reference program's by a relative error of at most 0.0065.
Values may be sent and summed in bfloat16 or wider, within the bound.
A program may use at most 128 MiB of HBM per device.

```python
import jax
import jax.numpy as jnp
import numpy as np
from jax import lax

NCOL = 1024
SL = 512
A_DEV = 2
TILES = 192
ANGLES = 512
NV = 32768
RAYB = 256
VB = 256
N_ANGLE = 16
N_PANEL = 16


def draw_live_tiles(key, part):
    counts = jax.random.randint(jax.random.fold_in(key, 11), (N_PANEL,), max(1, TILES // 4), TILES + 1)
    fullest = jax.random.randint(jax.random.fold_in(key, 12), (), 0, N_PANEL)
    return jnp.where(jnp.arange(N_PANEL) == fullest, TILES, counts).astype(jnp.int32)


def with_ends(values, stream_key, least, largest):
    dims = values.shape
    place = [jax.random.randint(jax.random.fold_in(stream_key, axis), (), 0, dims[axis]) for axis in range(len(dims))]
    values = values.at[tuple(place)].set(least)
    longest = dims.index(max(dims))
    place[longest] = (place[longest] + 1) % dims[longest]
    return values.at[tuple(place)].set(largest)


def steps_of(own_key, shape, split, smallest, largest):
    def one(axis_at, shards_of):
        steps = jax.random.uniform(jax.random.fold_in(jax.random.fold_in(own_key, 6), axis_at), (shards_of,), jnp.float32, smallest / len(split), largest / len(split))
        return jnp.repeat(jnp.exp(steps), shape[axis_at] // shards_of).reshape((-1,) + (1,) * (len(shape) - axis_at - 1))

    level = one(*split[0])
    for cut in split[1:]:
        level = level * one(*cut)
    return level


def centred(key, shape, spread, limit, shards=(), held_as=jnp.bfloat16):
    level = steps_of(key, shape, shards, -0.22, 0.18) if shards else 1.0
    values = jax.random.normal(key, shape, jnp.float32) * spread * level
    return jnp.minimum(jnp.maximum(values, -limit), limit).astype(held_as)


def setup_inputs(seed: int = 0) -> dict:
    streams_of = jax.random.split(jax.random.key(seed), 10)
    measured = jnp.clip(0.099609375 + 0.9003906 * jax.random.uniform(streams_of[0], (ANGLES, SL, NCOL), jnp.float32) ** steps_of(streams_of[0], (ANGLES, SL, NCOL), ((0, 256),), -0.2, 0.2), 0.099609375, 1.0).astype(jnp.bfloat16)
    predicted = jnp.clip(2.0 * jax.random.uniform(streams_of[1], (ANGLES, SL, NCOL), jnp.float32) ** steps_of(streams_of[1], (ANGLES, SL, NCOL), ((0, 256),), -0.2, 0.2), 0.0, 2.0).astype(jnp.bfloat16)
    slice_filter = centred(streams_of[2], (SL, SL), SL ** -0.5, 0.25)
    column_filter = centred(streams_of[3], (NCOL, NCOL), NCOL ** -0.5, 0.1875)
    volume = jnp.clip(1.0 * jax.random.uniform(streams_of[4], (SL, NV), jnp.float32) ** steps_of(streams_of[4], (SL, NV), ((0, 16), (1, 16)), -0.2, 0.2), 0.0, 1.0)
    tiles = centred(streams_of[5], (N_PANEL * TILES, 128, 128), 128 ** -0.5, 0.5, ((0, 16),))
    tile_ray = with_ends(jax.random.randint(streams_of[6], (N_PANEL * TILES,), 0, RAYB), jax.random.fold_in(streams_of[6], 1), 0, RAYB - 1).astype(jnp.int32)
    tile_vox = with_ends(jax.random.randint(streams_of[7], (N_PANEL * TILES,), 0, VB), jax.random.fold_in(streams_of[7], 1), 0, VB - 1).astype(jnp.int32)
    live_tiles = draw_live_tiles(jax.random.fold_in(streams_of[9], 71), 0)
    return {"measured": measured, "predicted": predicted, "slice_filter": slice_filter, "column_filter": column_filter, "volume": volume, "tiles": tiles, "tile_ray": tile_ray, "tile_vox": tile_vox, "live_tiles": live_tiles}


step_size = 0.1


def panel_angles(panel):
    listed = [(outer * N_PANEL + panel) * A_DEV + inner for outer in range(N_ANGLE) for inner in range(A_DEV)]
    return jnp.asarray(np.array(listed, dtype=np.int32))


def reference(measured, predicted, slice_filter, column_filter, volume, tiles, tile_ray, tile_vox, live_tiles):
    bright = jnp.exp(-predicted.astype(jnp.float32))
    misfit = ((measured.astype(jnp.float32) - bright) * bright).astype(jnp.bfloat16)
    across = jnp.dot(misfit.reshape(-1, NCOL), column_filter, preferred_element_type=jnp.float32)
    across = across.astype(jnp.bfloat16).reshape(misfit.shape)
    filtered = lax.map(lambda angle_plane: jnp.dot(slice_filter, angle_plane, preferred_element_type=jnp.float32).astype(jnp.bfloat16), across)
    col_blocks = NCOL // 128
    voxel_blocks = NV // 128
    local_angles = A_DEV * N_ANGLE
    gradient = jnp.zeros((SL, voxel_blocks, 128), jnp.float32)
    for panel in range(N_PANEL):
        angles = panel_angles(panel)
        ray_grid = filtered[angles].reshape(local_angles, SL, col_blocks, 128)
        ray_ids = tile_ray[panel * TILES:(panel + 1) * TILES].astype(jnp.int32)
        vox_ids = tile_vox[panel * TILES:(panel + 1) * TILES].astype(jnp.int32)
        panel_tiles = tiles[panel * TILES:(panel + 1) * TILES].astype(jnp.float32)
        active = jnp.arange(TILES) < live_tiles[panel]
        picked = ray_grid[ray_ids // col_blocks, :, ray_ids % col_blocks, :].astype(jnp.float32)
        contrib = jnp.einsum('tsr,trv->stv', picked, panel_tiles)
        contrib = jnp.where(active[None, :, None], contrib, jnp.float32(0.0))
        gradient = gradient.at[:, vox_ids, :].add(contrib)
    updated = jnp.clip(volume + step_size * gradient.reshape(SL, NV), 0.0, 1.0)
    voxels = updated.astype(jnp.bfloat16).reshape(SL, voxel_blocks, 128)
    projected = jnp.zeros((ANGLES, SL, NCOL), jnp.bfloat16)
    for panel in range(N_PANEL):
        angles = panel_angles(panel)
        ray_ids = tile_ray[panel * TILES:(panel + 1) * TILES].astype(jnp.int32)
        vox_ids = tile_vox[panel * TILES:(panel + 1) * TILES].astype(jnp.int32)
        panel_tiles = tiles[panel * TILES:(panel + 1) * TILES].astype(jnp.float32)
        active = jnp.arange(TILES) < live_tiles[panel]
        picked = voxels[:, vox_ids, :].astype(jnp.float32)
        contrib = jnp.einsum('stv,trv->tsr', picked, panel_tiles)
        contrib = jnp.where(active[:, None, None], contrib, jnp.float32(0.0))
        summed = jnp.zeros((local_angles, SL, col_blocks, 128), jnp.float32)
        summed = summed.at[ray_ids // col_blocks, :, ray_ids % col_blocks, :].add(contrib)
        projected = projected.at[angles].set(summed.astype(jnp.bfloat16).reshape(local_angles, SL, NCOL))
    return updated, projected
```

```python
import functools

import jax
import jax.numpy as jnp
from jax import lax
from jax.experimental import pallas as pl
from jax.experimental.pallas import tpu as pltpu
from jax.sharding import PartitionSpec as P

MESH = pl.DeviceIdType.MESH
BF = jnp.bfloat16
F32 = jnp.float32
I32 = jnp.int32
PLANE = 16
NZ = 8
SLOTS = 192
UNROLL = 32
STEP_SIZE = 0.1
NC = 2
R = 32 // NC


def kernel(
    measured, predicted, sfilt, cfilt, volume, tiles_hbm, ray_ref, vox_ref, live_ref,
    new_out, proj_out,
    m_v, p_v, sf_v, cf_v, vol_v, tiles, misfit, across, newvol,
    keys, idx_v, idx, *rest,
):
    names = (
        "filt", "gath", "slots", "sib_out", "sib_in", "part", "near", "far", "half", "mid", "mid2",
        "vox", "fslots", "stage",
    )
    per_chunk = len(names)
    bufs = [dict(zip(names, rest[c * per_chunk:(c + 1) * per_chunk])) for c in range(NC)]
    (in_sem, idx_sem, a_send, a_recv, sib_send, sib_recv, rs_send, rs_recv,
     ag_send, ag_recv, c_send, c_recv, loc_sem) = rest[NC * per_chunk:]

    a = lax.axis_index("angle")
    pan = lax.axis_index("panel")
    z = pan // 2
    core = pan % 2
    ax, ay = a % 4, a // 4

    def plane_peer(i):
        return ((ay + i // 4) % 4) * 4 + (ax + i) % 4

    def along_z(dz):
        return {"panel": ((z + dz + NZ) % NZ) * 2 + core}

    sibling = {"panel": z * 2 + (1 - core)}

    loads = [
        pltpu.make_async_copy(src, dst, in_sem.at[i])
        for i, (src, dst) in enumerate((
            (predicted.at[0], p_v.at[0]), (measured.at[0], m_v.at[0]), (cfilt, cf_v), (sfilt, sf_v),
            (predicted.at[1], p_v.at[1]), (measured.at[1], m_v.at[1]), (tiles_hbm, tiles), (volume, vol_v),
        ))
    ]
    for load in loads:
        load.start()

    barrier = pltpu.get_barrier_semaphore()

    @pl.loop(1, PLANE)
    def _(i):
        pl.semaphore_signal(barrier, inc=1, device_id={"angle": plane_peer(i)}, device_id_type=MESH)

    for peer in (sibling, along_z(1), along_z(-1), along_z(2), along_z(-2)):
        pl.semaphore_signal(barrier, inc=1, device_id=peer, device_id_type=MESH)

    def misfit_of(k):
        @pl.loop(0, 8)
        def _(i):
            rows = pl.ds(pl.multiple_of(i * 64, 64), 64)
            bright = jnp.exp(-p_v[k, rows, :].astype(F32))
            misfit[rows, :] = ((m_v[k, rows, :].astype(F32) - bright) * bright).astype(BF)

    def across_of(k):
        @pl.loop(0, 4)
        def _(n):
            columns = pl.ds(pl.multiple_of(n * 256, 256), 256)
            across[k, n] = jnp.dot(misfit[...], cf_v[:, columns], preferred_element_type=F32).astype(BF)

    def filter_of(c, k):
        filt = bufs[c]["filt"]

        @pl.loop(0, 4)
        def _(n):
            rows = sf_v[:, c].reshape(PLANE * R, 512)
            out = jnp.dot(rows, across[k, n], preferred_element_type=F32).astype(BF)
            for d in range(PLANE):
                for j in range(2):
                    filt[d * 16 + k * 8 + n * 2 + j] = out[d * R:(d + 1) * R, j * 128:(j + 1) * 128]

    def send_filtered(c):
        filt, gath = bufs[c]["filt"], bufs[c]["gath"]

        @pl.loop(1, PLANE)
        def _(i):
            peer = plane_peer(i)
            pltpu.make_async_remote_copy(
                src_ref=filt.at[pl.ds(peer * 16, 16)],
                dst_ref=gath.at[pl.ds(a * 16, 16)],
                send_sem=a_send.at[c], recv_sem=a_recv.at[c],
                device_id={"angle": peer}, device_id_type=MESH,
            ).start()

        gath[pl.ds(a * 16, 16)] = filt[pl.ds(a * 16, 16)]

    def wait_bytes(ref, sem):
        pltpu.make_async_copy(ref, ref, sem).wait()

    def remote(src, dst, send, recv, device):
        pltpu.make_async_remote_copy(
            src_ref=src, dst_ref=dst, send_sem=send, recv_sem=recv, device_id=device, device_id_type=MESH
        ).start()

    def order_tiles():
        row = lax.broadcasted_iota(I32, (256, 256), 0)
        col = lax.broadcasted_iota(I32, (256, 256), 1)
        dead = 256
        keys[...] = jnp.full((8, 256), dead, I32)
        keys[0:1, 0:SLOTS] = vox_ref[...]
        keys[1:2, 0:SLOTS] = ray_ref[...]
        live = live_ref[0]

        def down(x):
            return jnp.sum(x, axis=0, keepdims=True)

        def spread(x):
            return jnp.broadcast_to(x, (256, 256))

        def one(main, other, at, address):
            main_row = spread(main)
            main_row = jnp.where(col < live, main_row, dead)
            main_col = main_row.T
            other_col = spread(other).T
            same_before = ((main_col == main_row) & (row < col)).astype(I32)
            before = same_before + (main_col < main_row).astype(I32)
            rank_col = spread(down(before)).T
            repeat_col = spread((down(same_before) > 0).astype(I32)).T
            placed = (rank_col == col).astype(I32)
            idx_v[at:at + 1, :] = down(placed * row)
            idx_v[at + 1:at + 2, :] = address(down(placed * other_col))
            idx_v[at + 2:at + 3, :] = down(placed * repeat_col)
            through = down((main_col <= col).astype(I32)) - 1
            present = down((main_col == col).astype(I32)) > 0
            idx_v[at + 3:at + 4, :] = jnp.where(present, through, SLOTS)

        def voxel_address(v):
            block_z, block_core = (v >> 5) & 7, (v >> 4) & 1
            return block_core * 128 + ((block_z - z + 10) & 7) * 16 + (v & 15)

        one(keys[0:1, :], keys[1:2, :], 0, lambda r: r & 255)
        one(keys[1:2, :], keys[0:1, :], 4, voxel_address)
        move = pltpu.make_async_copy(idx_v, idx, idx_sem)
        move.start()
        move.wait()

    def tile_sums(source, slots, at, transposed):
        slots[SLOTS] = jnp.zeros((R, 128), BF)
        blank = jnp.zeros((R, 128), BF)
        joined = 0 if transposed else 1
        contract = (((1,), (1,)), ((), ())) if transposed else (((1,), (0,)), ((), ()))

        def four(j, acc):
            ts = [tiles[idx[at, j + i]] for i in range(4)]
            xs = [source[idx[at + 1, j + i]] for i in range(4)]
            left = jnp.concatenate(
                [jnp.concatenate([xs[0], blank], 1), jnp.concatenate([xs[1], blank], 1),
                 jnp.concatenate([blank, xs[2]], 1), jnp.concatenate([blank, xs[3]], 1)], 0)
            right = jnp.concatenate(
                [jnp.concatenate(ts[:2], joined), jnp.concatenate(ts[2:], joined)], 1 - joined)
            out = lax.dot_general(left, right, contract, preferred_element_type=F32)
            for i in range(4):
                lane = (i % 2) * 128
                term = out[i * R:(i + 1) * R, lane:lane + 128]
                acc = acc * idx[at + 2, j + i].astype(F32) + term
                slots[j + i] = acc.astype(BF)
            return acc

        def body(step, acc):
            for u in range(UNROLL // 4):
                acc = four(step * UNROLL + u * 4, acc)
            return acc

        lax.fori_loop(0, SLOTS // UNROLL, body, jnp.zeros((R, 128), F32))

    def panel_block(rel, which):
        return (((z + rel + 6) % NZ) * 2 + which) * 16

    def share(rel):
        return pl.ds(rel * 16, 16)

    def collect_for_sibling(c, first, count):
        b = bufs[c]

        @pl.loop(0, count)
        def _(o):
            base = panel_block(first + o, 1 - core)
            for i in range(16):
                b["sib_out"][(first + o) * 16 + i] = b["slots"][idx[3, base + i]]

    def send_to_sibling(c, part, first, count):
        b = bufs[c]
        where = pl.ds(first * 16, count * 16)
        remote(b["sib_out"].at[where], b["sib_in"].at[where], sib_send.at[c], sib_recv.at[c, part], sibling)

    def back_project(c):
        b = bufs[c]
        wait_bytes(b["gath"].at[pl.ds(0, 240)], a_recv.at[c])
        tile_sums(b["gath"], b["slots"], 0, False)
        collect_for_sibling(c, 5, 3)
        send_to_sibling(c, 0, 5, 3)
        collect_for_sibling(c, 0, 5)
        send_to_sibling(c, 1, 0, 5)

    def wait_sibling(c, part, first, count):
        where = pl.ds(first * 16, count * 16)
        wait_bytes(bufs[c]["sib_in"].at[where], sib_recv.at[c, part])

    def pair_sum(c, rel, i):
        b = bufs[c]
        own = b["slots"][idx[3, panel_block(rel, core) + i]]
        return own.astype(F32) + b["sib_in"][rel * 16 + i].astype(F32)

    def make_part(c, rel):
        part = bufs[c]["part"]
        for i in range(16):
            part[rel * 16 + i] = pair_sum(c, rel, i).astype(BF)

    def reduce_first(c):
        b = bufs[c]
        wait_sibling(c, 0, 5, 3)
        for rel in (5, 7, 6):
            make_part(c, rel)
        for way, sign, far_rel in ((0, 1, 5), (1, -1, 7)):
            remote(b["part"].at[share(far_rel)], b["far"].at[way], rs_send.at[c], rs_recv.at[c, way], along_z(sign))
            half = pl.ds(6 * 16 + way * 8, 8)
            remote(b["part"].at[half], b["half"].at[way], rs_send.at[c], rs_recv.at[c, 2 + way], along_z(2 * sign))
        wait_sibling(c, 1, 0, 5)
        for way, sign, rel in ((0, 1, 3), (1, -1, 1)):
            make_part(c, rel)
            remote(b["part"].at[share(rel)], b["near"].at[way], rs_send.at[c], rs_recv.at[c, 4 + way], along_z(sign))

    def reduce_second(c):
        b = bufs[c]
        for way, sign, rel in ((0, 1, 4), (1, -1, 0)):
            wait_bytes(b["far"].at[way], rs_recv.at[c, way])
            wait_bytes(b["half"].at[way], rs_recv.at[c, 2 + way])
            for i in range(16):
                total = pair_sum(c, rel, i) + b["far"][way, i].astype(F32)
                if i // 8 == way:
                    total = total + b["half"][way, i % 8].astype(F32)
                b["mid"][way, i] = total.astype(BF)
            remote(b["mid"].at[way], b["mid2"].at[way], rs_send.at[c], rs_recv.at[c, 6 + way], along_z(2 * sign))

    def update(c):
        b = bufs[c]
        for way in range(2):
            wait_bytes(b["near"].at[way], rs_recv.at[c, 4 + way])
            wait_bytes(b["mid2"].at[way], rs_recv.at[c, 6 + way])
        mine = core * 128 + 2 * 16
        for i in range(16):
            total = pair_sum(c, 2, i)
            for way in range(2):
                total = total + b["near"][way, i].astype(F32) + b["mid2"][way, i].astype(F32)
            lanes = slice(i * 128, (i + 1) * 128)
            new = jnp.clip(vol_v[c, :, lanes] + STEP_SIZE * total, 0.0, 1.0)
            newvol[c, :, lanes] = new
            b["vox"][mine + i] = new.astype(BF)
        base = core * 128
        own = b["vox"].at[pl.ds(mine, 16)]
        for n, (dz, rel) in enumerate(((2, 0), (-2, 4), (1, 1), (-1, 3))):
            remote(own, b["vox"].at[pl.ds(base + rel * 16, 16)], ag_send.at[c], ag_recv.at[c, n], along_z(dz))
        pltpu.make_async_copy(newvol.at[c], new_out.at[c], loc_sem.at[c]).start()

    def gather_second(c):
        b = bufs[c]
        base = core * 128
        vox = b["vox"]
        for way, sign, came, goes in ((0, 1, 0, 7), (1, -1, 4, 5)):
            block = vox.at[pl.ds(base + came * 16, 16)]
            wait_bytes(block, ag_recv.at[c, way])
            remote(block, vox.at[pl.ds(base + goes * 16, 16)], ag_send.at[c], ag_recv.at[c, 4 + way], along_z(sign))
            remote(
                vox.at[pl.ds(base + came * 16 + way * 8, 8)], vox.at[pl.ds(base + 6 * 16 + way * 8, 8)],
                ag_send.at[c], ag_recv.at[c, 6 + way], along_z(2 * sign))
        for n, rel in ((2, 1), (3, 3)):
            wait_bytes(vox.at[pl.ds(base + rel * 16, 16)], ag_recv.at[c, n])
        first = vox.at[pl.ds(base, 80)]
        remote(first, first, ag_send.at[c], sib_recv.at[c, 2], sibling)

    def gather_third(c):
        vox = bufs[c]["vox"]
        base = core * 128
        for way, goes in ((0, 7), (1, 5)):
            wait_bytes(vox.at[pl.ds(base + goes * 16, 16)], ag_recv.at[c, 4 + way])
            wait_bytes(vox.at[pl.ds(base + 6 * 16 + way * 8, 8)], ag_recv.at[c, 6 + way])
        last = vox.at[pl.ds(base + 80, 48)]
        remote(last, last, ag_send.at[c], sib_recv.at[c, 3], sibling)

    def project(c):
        b = bufs[c]
        vox, stage, fslots = b["vox"], b["stage"], b["fslots"]
        other = (1 - core) * 128
        wait_bytes(vox.at[pl.ds(other, 80)], sib_recv.at[c, 2])
        wait_bytes(vox.at[pl.ds(other + 80, 48)], sib_recv.at[c, 3])
        tile_sums(vox, fslots, 4, True)

        @pl.loop(0, 32)
        def _(k):
            for j in range(8):
                stage[k, :, j * 128:(j + 1) * 128] = fslots[idx[7, k * 8 + j]]

        @pl.loop(1, PLANE)
        def _(i):
            peer = plane_peer(i)
            remote(stage.at[pl.ds(peer * 2, 2)], proj_out.at[:, a, c], c_send.at[c], c_recv.at[c], {"angle": peer})

        pltpu.make_async_copy(stage.at[pl.ds(a * 2, 2)], proj_out.at[:, a, c], loc_sem.at[NC + c]).start()

    loads[0].wait()
    loads[1].wait()
    misfit_of(0)
    loads[2].wait()
    across_of(0)
    loads[3].wait()
    filter_of(0, 0)
    loads[4].wait()
    loads[5].wait()
    misfit_of(1)
    across_of(1)
    filter_of(0, 1)
    pl.semaphore_wait(barrier, PLANE - 1 + 5)
    send_filtered(0)
    for c in range(1, NC):
        for k in range(2):
            filter_of(c, k)
        send_filtered(c)
    order_tiles()
    loads[6].wait()
    loads[7].wait()

    back_project(0)
    reduce_first(0)
    reduce_second(0)
    back_project(1)
    update(0)
    reduce_first(1)
    gather_second(0)
    reduce_second(1)
    gather_third(0)
    project(0)
    update(1)
    gather_second(1)
    gather_third(1)
    project(1)

    for c in range(NC):
        b = bufs[c]
        wait_bytes(b["filt"].at[pl.ds(0, 240)], a_send.at[c])
        wait_bytes(b["sib_out"], sib_send.at[c])
        wait_bytes(b["vox"].at[pl.ds(0, 112)], rs_send.at[c])
        wait_bytes(b["vox"].at[pl.ds(0, 112 + 128)], ag_send.at[c])
        pltpu.make_async_copy(newvol.at[c], new_out.at[c], loc_sem.at[c]).wait()
        pltpu.make_async_copy(stage_of(b, a), proj_out.at[:, a, c], loc_sem.at[NC + c]).wait()
        wait_bytes(b["stage"].at[pl.ds(0, 30)], c_send.at[c])
        wait_bytes(b["stage"].at[pl.ds(0, 30)], c_recv.at[c])


def stage_of(b, a):
    return b["stage"].at[pl.ds(a * 2, 2)]


def per_device(measured, predicted, slice_filter, column_filter, volume, tiles, tile_ray, tile_vox, live_tiles):
    V = pltpu.VMEM
    D = pltpu.SemaphoreType.DMA
    share = (16, R, 128)
    chunk_scratch = [
        V((256, R, 128), BF),
        V((256, R, 128), BF),
        V((SLOTS + 1, R, 128), BF),
        V((128, R, 128), BF),
        V((128, R, 128), BF),
        V((128, R, 128), BF),
        V((2,) + share, BF),
        V((2,) + share, BF),
        V((2, 8, R, 128), BF),
        V((2,) + share, BF),
        V((2,) + share, BF),
        V((256, R, 128), BF),
        V((SLOTS + 1, R, 128), BF),
        V((32, R, 1024), BF),
    ]
    scratch = [
        V((2, 512, 1024), BF), V((2, 512, 1024), BF), V((PLANE, NC, R, 512), BF), V((1024, 1024), BF),
        V((NC, R, 2048), F32), V((SLOTS, 128, 128), BF), V((512, 1024), BF), V((2, 4, 512, 256), BF),
        V((NC, R, 2048), F32), V((8, 256), I32), V((8, 256), I32), pltpu.SMEM((8, 256), I32),
    ] + chunk_scratch * NC + [
        D((8,)), D, D((NC,)), D((NC,)), D((NC,)), D((NC, 4)), D((NC,)), D((NC, 8)),
        D((NC,)), D((NC, 8)), D((NC,)), D((NC,)), D((2 * NC,)),
    ]
    hbm = pl.BlockSpec(memory_space=pl.ANY)
    vmem = pl.BlockSpec(memory_space=pltpu.VMEM)
    new_share, projected = pl.pallas_call(
        kernel,
        out_shape=(
            jax.ShapeDtypeStruct((NC, R, 2048), F32),
            jax.ShapeDtypeStruct((2, PLANE, NC, R, 1024), BF),
        ),
        in_specs=[hbm] * 6 + [vmem, vmem, pl.BlockSpec(memory_space=pltpu.SMEM)],
        out_specs=(hbm, hbm),
        scratch_shapes=scratch,
        compiler_params=pltpu.CompilerParams(
            collective_id=0, has_side_effects=True, vmem_limit_bytes=60 * 1024 * 1024
        ),
        name="tomography_iteration",
    )(
        measured, predicted, slice_filter.reshape(PLANE, NC, R, 512), column_filter,
        volume.reshape(NC, R, 2048), tiles, tile_ray.reshape(1, SLOTS), tile_vox.reshape(1, SLOTS), live_tiles,
    )
    return new_share.reshape(NC * R, 2048), projected.reshape(2, 512, 1024)


def solution(mesh):
    split = P(("angle", "panel"), None, None)
    return jax.shard_map(
        per_device,
        mesh=mesh,
        in_specs=(
            split, split, P(), P(), P("angle", "panel"), P("panel", None, None), P("panel"), P("panel"), P("panel"),
        ),
        out_specs=(P("angle", "panel"), split),
        check_vma=False,
    )
```

```python
import functools

import jax
import jax.numpy as jnp
from jax import lax
from jax.experimental import pallas as pl
from jax.experimental.pallas import tpu as pltpu
from jax.sharding import PartitionSpec as P

MESH = pl.DeviceIdType.MESH
BF = jnp.bfloat16
F32 = jnp.float32
I32 = jnp.int32
PLANE = 16
NZ = 8
SLOTS = 192
UNROLL = 96
STEP_SIZE = 0.1
ACROSS_UNROLL = 2
SPLIT_ANGLES = True
UNIT = 8
UNITS = (1, 1, 1, 1)
NC = len(UNITS)
SCHEDULE = (
    "B0 10 B1 20", "11 U0 B2 21", "12 30 U1 B3", "22 40 13 31", "U2 23 P0 32", "41 U3 P1 42", "33 P2 43 P3",
)
FIRST = tuple(sum(UNITS[:c]) for c in range(NC))


def kernel(
    measured, predicted, sfilt, cfilt, volume, tiles_hbm, ray_hbm, vox_hbm, live_ref,
    new_out, proj_out,
    m_v, p_v, sf_v, cf_v, vol_v, tiles, misfit, across, newvol,
    keys, ray_v, vox_v, idx_v, idx, *rest,
):
    names = (
        "filt", "gath", "slots", "sib_out", "sib_in", "part", "near", "far", "half", "mid", "mid2",
        "vox", "fslots", "stage",
    )
    per_chunk = len(names)
    bufs = [dict(zip(names, rest[c * per_chunk:(c + 1) * per_chunk])) for c in range(NC)]
    (in_sem, idx_sem, a_send, a_recv, sib_send, sib_recv, rs_send, rs_recv,
     ag_send, ag_recv, c_send, c_recv, loc_sem) = rest[NC * per_chunk:]

    a = lax.axis_index("angle")
    pan = lax.axis_index("panel")
    z = pan // 2
    core = pan % 2
    ax, ay = a % 4, a // 4

    def plane_peer(i):
        return ((ay + i // 4) % 4) * 4 + (ax + i) % 4

    def along_z(dz):
        return {"panel": ((z + dz + NZ) % NZ) * 2 + core}

    def units_of(c):
        return pl.ds(FIRST[c], UNITS[c])

    def volume_store(c):
        return pltpu.make_async_copy(newvol.at[units_of(c)], new_out.at[units_of(c)], loc_sem.at[c])

    def own_projection(c):
        return pltpu.make_async_copy(
            bufs[c]["stage"].at[pl.ds(a * 2, 2)], proj_out.at[:, a, units_of(c)], loc_sem.at[NC + c])

    sibling = {"panel": z * 2 + (1 - core)}

    loads = [
        pltpu.make_async_copy(src, dst, in_sem.at[i])
        for i, (src, dst) in enumerate((
            (predicted.at[0], p_v.at[0]), (measured.at[0], m_v.at[0]), (cfilt, cf_v), (sfilt, sf_v),
            (predicted.at[1], p_v.at[1]), (measured.at[1], m_v.at[1]), (tiles_hbm, tiles), (volume, vol_v), (ray_hbm, ray_v), (vox_hbm, vox_v),
        ))
    ]
    for load in loads[:6]:
        load.start()

    barrier = pltpu.get_barrier_semaphore()

    @pl.loop(1, PLANE)
    def _(i):
        pl.semaphore_signal(barrier, inc=1, device_id={"angle": plane_peer(i)}, device_id_type=MESH)

    for peer in (sibling, along_z(1), along_z(-1), along_z(2), along_z(-2)):
        pl.semaphore_signal(barrier, inc=1, device_id=peer, device_id_type=MESH)

    def misfit_of(k):
        @pl.loop(0, 8)
        def _(i):
            rows = pl.ds(pl.multiple_of(i * 64, 64), 64)
            bright = jnp.exp(-p_v[k, rows, :].astype(F32))
            misfit[rows, :] = ((m_v[k, rows, :].astype(F32) - bright) * bright).astype(BF)

    def across_of(k):
        @pl.loop(0, 4 // ACROSS_UNROLL)
        def _(step):
            for u in range(ACROSS_UNROLL):
                n = step * ACROSS_UNROLL + u
                columns = pl.ds(pl.multiple_of(n * 256, 256), 256)
                across[k, n] = jnp.dot(misfit[...], cf_v[:, columns], preferred_element_type=F32).astype(BF)

    def filter_of(c, k):
        filt = bufs[c]["filt"]
        r = UNITS[c] * UNIT

        rows = sf_v[:, FIRST[c]:FIRST[c] + UNITS[c]].reshape(PLANE * r, 512)
        for n in range(4):
            out = jnp.dot(rows, across[k, n], preferred_element_type=F32).astype(BF)
            for d in range(PLANE):
                for j in range(2):
                    filt[d * 16 + k * 8 + n * 2 + j] = out[d * r:(d + 1) * r, j * 128:(j + 1) * 128]

    def send_filtered(c, at=0, count=16):
        filt, gath = bufs[c]["filt"], bufs[c]["gath"]

        @pl.loop(1, PLANE)
        def _(i):
            peer = plane_peer(i)
            pltpu.make_async_remote_copy(
                src_ref=filt.at[pl.ds(peer * 16 + at, count)],
                dst_ref=gath.at[pl.ds(a * 16 + at, count)],
                send_sem=a_send.at[c], recv_sem=a_recv.at[c],
                device_id={"angle": peer}, device_id_type=MESH,
            ).start()

        gath[pl.ds(a * 16 + at, count)] = filt[pl.ds(a * 16 + at, count)]

    def wait_bytes(ref, sem):
        pltpu.make_async_copy(ref, ref, sem).wait()

    def remote(src, dst, send, recv, device):
        pltpu.make_async_remote_copy(
            src_ref=src, dst_ref=dst, send_sem=send, recv_sem=recv, device_id=device, device_id_type=MESH
        ).start()

    def order_tiles():
        row = lax.broadcasted_iota(I32, (256, 256), 0)
        col = lax.broadcasted_iota(I32, (256, 256), 1)
        dead = 256
        keys[...] = jnp.full((8, 256), dead, I32)
        keys[0:1, 0:SLOTS] = vox_v[...]
        keys[1:2, 0:SLOTS] = ray_v[...]
        live = live_ref[0]

        def down(x):
            return jnp.sum(x, axis=0, keepdims=True)

        def spread(x):
            return jnp.broadcast_to(x, (256, 256))

        def one(main, other, at, address):
            main_row = spread(main)
            main_row = jnp.where(col < live, main_row, dead)
            main_col = main_row.T
            other_col = spread(other).T
            same_before = ((main_col == main_row) & (row < col)).astype(I32)
            before = same_before + (main_col < main_row).astype(I32)
            rank_col = spread(down(before)).T
            repeat_col = spread((down(same_before) > 0).astype(I32)).T
            placed = (rank_col == col).astype(I32)
            idx_v[at:at + 1, :] = down(placed * row)
            idx_v[at + 1:at + 2, :] = address(down(placed * other_col))
            idx_v[at + 2:at + 3, :] = down(placed * repeat_col)
            through = down((main_col <= col).astype(I32)) - 1
            present = down((main_col == col).astype(I32)) > 0
            idx_v[at + 3:at + 4, :] = jnp.where(present, through, SLOTS)

        def voxel_address(v):
            block_z, block_core = (v >> 5) & 7, (v >> 4) & 1
            return block_core * 128 + ((block_z - z + 10) & 7) * 16 + (v & 15)

        one(keys[0:1, :], keys[1:2, :], 0, lambda r: r & 255)
        one(keys[1:2, :], keys[0:1, :], 4, voxel_address)
        move = pltpu.make_async_copy(idx_v, idx, idx_sem)
        move.start()
        move.wait()

    def tile_sums(c, source, slots, at, transposed):
        r = UNITS[c] * UNIT
        blank = jnp.zeros((r, 128), BF)
        slots[SLOTS] = blank
        joined = 0 if transposed else 1
        contract = (((1,), (1,)), ((), ())) if transposed else (((1,), (0,)), ((), ()))

        def four(j, acc):
            ts = [tiles[idx[at, j + i]] for i in range(4)]
            xs = [source[idx[at + 1, j + i]] for i in range(4)]
            left = jnp.concatenate(
                [jnp.concatenate([xs[0], blank], 1), jnp.concatenate([xs[1], blank], 1),
                 jnp.concatenate([blank, xs[2]], 1), jnp.concatenate([blank, xs[3]], 1)], 0)
            right = jnp.concatenate(
                [jnp.concatenate(ts[:2], joined), jnp.concatenate(ts[2:], joined)], 1 - joined)
            out = lax.dot_general(left, right, contract, preferred_element_type=F32)
            for i in range(4):
                lane = (i % 2) * 128
                term = out[i * r:(i + 1) * r, lane:lane + 128]
                acc = acc * idx[at + 2, j + i].astype(F32) + term
                slots[j + i] = acc.astype(BF)
            return acc

        def body(step, acc):
            for u in range(UNROLL // 4):
                acc = four(step * UNROLL + u * 4, acc)
            return acc

        lax.fori_loop(0, SLOTS // UNROLL, body, jnp.zeros((r, 128), F32))

    def panel_block(rel, which):
        return (((z + rel + 6) % NZ) * 2 + which) * 16

    def share(rel):
        return pl.ds(rel * 16, 16)

    def collect_for_sibling(c, first, count):
        b = bufs[c]

        @pl.loop(0, count)
        def _(o):
            base = panel_block(first + o, 1 - core)
            for i in range(16):
                b["sib_out"][(first + o) * 16 + i] = b["slots"][idx[3, base + i]]

    def send_to_sibling(c, part, first, count):
        b = bufs[c]
        where = pl.ds(first * 16, count * 16)
        remote(b["sib_out"].at[where], b["sib_in"].at[where], sib_send.at[c], sib_recv.at[c, part], sibling)

    def back_project(c):
        b = bufs[c]
        wait_bytes(b["gath"].at[pl.ds(0, 240)], a_recv.at[c])
        tile_sums(c, b["gath"], b["slots"], 0, False)
        collect_for_sibling(c, 5, 3)
        send_to_sibling(c, 0, 5, 3)
        collect_for_sibling(c, 0, 5)
        send_to_sibling(c, 1, 0, 5)

    def wait_sibling(c, part, first, count):
        where = pl.ds(first * 16, count * 16)
        wait_bytes(bufs[c]["sib_in"].at[where], sib_recv.at[c, part])

    def pair_sum(c, rel, i):
        b = bufs[c]
        own = b["slots"][idx[3, panel_block(rel, core) + i]]
        return own.astype(F32) + b["sib_in"][rel * 16 + i].astype(F32)

    def make_part(c, rel):
        part = bufs[c]["part"]
        for i in range(16):
            part[rel * 16 + i] = pair_sum(c, rel, i).astype(BF)

    def reduce_first(c):
        b = bufs[c]
        wait_sibling(c, 0, 5, 3)
        for rel in (5, 7, 6):
            make_part(c, rel)
        for way, sign, far_rel in ((0, 1, 5), (1, -1, 7)):
            remote(b["part"].at[share(far_rel)], b["far"].at[way], rs_send.at[c], rs_recv.at[c, way], along_z(sign))
            half = pl.ds(6 * 16 + way * 8, 8)
            remote(b["part"].at[half], b["half"].at[way], rs_send.at[c], rs_recv.at[c, 2 + way], along_z(2 * sign))
        wait_sibling(c, 1, 0, 5)
        for way, sign, rel in ((0, 1, 3), (1, -1, 1)):
            make_part(c, rel)
            remote(b["part"].at[share(rel)], b["near"].at[way], rs_send.at[c], rs_recv.at[c, 4 + way], along_z(sign))

    def reduce_second(c):
        b = bufs[c]
        for way, sign, rel in ((0, 1, 4), (1, -1, 0)):
            wait_bytes(b["far"].at[way], rs_recv.at[c, way])
            wait_bytes(b["half"].at[way], rs_recv.at[c, 2 + way])
            for i in range(16):
                total = pair_sum(c, rel, i) + b["far"][way, i].astype(F32)
                if i // 8 == way:
                    total = total + b["half"][way, i % 8].astype(F32)
                b["mid"][way, i] = total.astype(BF)
            remote(b["mid"].at[way], b["mid2"].at[way], rs_send.at[c], rs_recv.at[c, 6 + way], along_z(2 * sign))

    def update(c):
        b = bufs[c]
        for way in range(2):
            wait_bytes(b["near"].at[way], rs_recv.at[c, 4 + way])
            wait_bytes(b["mid2"].at[way], rs_recv.at[c, 6 + way])
        mine = core * 128 + 2 * 16
        for i in range(16):
            total = pair_sum(c, 2, i)
            for way in range(2):
                total = total + b["near"][way, i].astype(F32) + b["mid2"][way, i].astype(F32)
            lanes = slice(i * 128, (i + 1) * 128)
            old = vol_v[units_of(c), :, lanes].reshape(UNITS[c] * UNIT, 128)
            new = jnp.clip(old + STEP_SIZE * total, 0.0, 1.0)
            newvol[units_of(c), :, lanes] = new.reshape(UNITS[c], UNIT, 128)
            b["vox"][mine + i] = new.astype(BF)
        base = core * 128
        own = b["vox"].at[pl.ds(mine, 16)]
        for n, (dz, rel) in enumerate(((2, 0), (-2, 4), (1, 1), (-1, 3))):
            remote(own, b["vox"].at[pl.ds(base + rel * 16, 16)], ag_send.at[c], ag_recv.at[c, n], along_z(dz))
        volume_store(c).start()

    def gather_second(c):
        b = bufs[c]
        base = core * 128
        vox = b["vox"]
        for way, sign, came, goes in ((0, 1, 0, 7), (1, -1, 4, 5)):
            block = vox.at[pl.ds(base + came * 16, 16)]
            wait_bytes(block, ag_recv.at[c, way])
            remote(block, vox.at[pl.ds(base + goes * 16, 16)], ag_send.at[c], ag_recv.at[c, 4 + way], along_z(sign))
            remote(
                vox.at[pl.ds(base + came * 16 + way * 8, 8)], vox.at[pl.ds(base + 6 * 16 + way * 8, 8)],
                ag_send.at[c], ag_recv.at[c, 6 + way], along_z(2 * sign))
        for n, rel in ((2, 1), (3, 3)):
            wait_bytes(vox.at[pl.ds(base + rel * 16, 16)], ag_recv.at[c, n])
        first = vox.at[pl.ds(base, 80)]
        remote(first, first, ag_send.at[c], sib_recv.at[c, 2], sibling)

    def gather_third(c):
        vox = bufs[c]["vox"]
        base = core * 128
        for way, goes in ((0, 7), (1, 5)):
            wait_bytes(vox.at[pl.ds(base + goes * 16, 16)], ag_recv.at[c, 4 + way])
            wait_bytes(vox.at[pl.ds(base + 6 * 16 + way * 8, 8)], ag_recv.at[c, 6 + way])
        last = vox.at[pl.ds(base + 80, 48)]
        remote(last, last, ag_send.at[c], sib_recv.at[c, 3], sibling)

    def project(c):
        b = bufs[c]
        vox, stage, fslots = b["vox"], b["stage"], b["fslots"]
        other = (1 - core) * 128
        wait_bytes(vox.at[pl.ds(other, 80)], sib_recv.at[c, 2])
        wait_bytes(vox.at[pl.ds(other + 80, 48)], sib_recv.at[c, 3])
        tile_sums(c, vox, fslots, 4, True)

        @pl.loop(0, 32)
        def _(k):
            for j in range(8):
                block = fslots[idx[7, k * 8 + j]]
                stage[k, :, :, j * 128:(j + 1) * 128] = block.reshape(UNITS[c], UNIT, 128)

        @pl.loop(1, PLANE)
        def _(i):
            peer = plane_peer(i)
            remote(stage.at[pl.ds(peer * 2, 2)], proj_out.at[:, a, units_of(c)], c_send.at[c], c_recv.at[c], {"angle": peer})

        own_projection(c).start()

    for load in loads[:2]:
        load.wait()
    misfit_of(0)
    loads[2].wait()
    across_of(0)
    loads[3].wait()
    for load in loads[6:]:
        load.start()
    filter_of(0, 0)
    pl.semaphore_wait(barrier, PLANE - 1 + 5)
    if SPLIT_ANGLES:
        send_filtered(0, 0, 8)
    for load in loads[4:6]:
        load.wait()
    misfit_of(1)
    across_of(1)
    filter_of(0, 1)
    if SPLIT_ANGLES:
        send_filtered(0, 8, 8)
    else:
        send_filtered(0)
    for c in range(1, NC):
        for k in range(2):
            filter_of(c, k)
        send_filtered(c)
    for load in loads[8:]:
        load.wait()
    order_tiles()
    for load in loads[6:8]:
        load.wait()

    stages = {
        "B": back_project, "1": reduce_first, "2": reduce_second, "U": update, "3": gather_second,
        "4": gather_third, "P": project,
    }
    for step in " ".join(SCHEDULE).split():
        stages[step[0]](int(step[1]))

    for c in range(NC):
        b = bufs[c]
        wait_bytes(b["filt"].at[pl.ds(0, 240)], a_send.at[c])
        wait_bytes(b["sib_out"], sib_send.at[c])
        wait_bytes(b["vox"].at[pl.ds(0, 112)], rs_send.at[c])
        wait_bytes(b["vox"].at[pl.ds(0, 112 + 128)], ag_send.at[c])
        volume_store(c).wait()
        own_projection(c).wait()
        wait_bytes(b["stage"].at[pl.ds(0, 30)], c_send.at[c])
        wait_bytes(b["stage"].at[pl.ds(0, 30)], c_recv.at[c])


def per_device(measured, predicted, slice_filter, column_filter, volume, tiles, tile_ray, tile_vox, live_tiles):
    V = pltpu.VMEM
    D = pltpu.SemaphoreType.DMA
    chunks = []
    for u in UNITS:
        r = u * UNIT
        share = (16, r, 128)
        chunks += [
            V((256, r, 128), BF),
            V((256, r, 128), BF),
            V((SLOTS + 1, r, 128), BF),
            V((128, r, 128), BF),
            V((128, r, 128), BF),
            V((128, r, 128), BF),
            V((2,) + share, BF),
            V((2,) + share, BF),
            V((2, 8, r, 128), BF),
            V((2,) + share, BF),
            V((2,) + share, BF),
            V((256, r, 128), BF),
            V((SLOTS + 1, r, 128), BF),
            V((32, u, UNIT, 1024), BF),
        ]
    scratch = [
        V((2, 512, 1024), BF), V((2, 512, 1024), BF), V((PLANE, 4, UNIT, 512), BF), V((1024, 1024), BF),
        V((4, UNIT, 2048), F32), V((SLOTS, 128, 128), BF), V((512, 1024), BF), V((2, 4, 512, 256), BF),
        V((4, UNIT, 2048), F32), V((8, 256), I32), V((1, SLOTS), I32), V((1, SLOTS), I32), V((8, 256), I32), pltpu.SMEM((8, 256), I32),
    ] + chunks + [
        D((10,)), D, D((NC,)), D((NC,)), D((NC,)), D((NC, 4)), D((NC,)), D((NC, 8)),
        D((NC,)), D((NC, 8)), D((NC,)), D((NC,)), D((2 * NC,)),
    ]
    anywhere = pl.BlockSpec(memory_space=pl.ANY)
    new_share, projected = pl.pallas_call(
        kernel,
        out_shape=(
            jax.ShapeDtypeStruct((4, UNIT, 2048), F32),
            jax.ShapeDtypeStruct((2, PLANE, 4, UNIT, 1024), BF),
        ),
        in_specs=[pl.BlockSpec(memory_space=pltpu.HBM)] * 8 + [pl.BlockSpec(memory_space=pltpu.SMEM)],
        out_specs=(anywhere, anywhere),
        scratch_shapes=scratch,
        compiler_params=pltpu.CompilerParams(
            collective_id=0, has_side_effects=True, vmem_limit_bytes=36 * 1024 * 1024
        ),
        name="tomography_iteration",
    )(*[pltpu.with_memory_space_constraint(x, pltpu.HBM) for x in (
        measured, predicted, slice_filter.reshape(PLANE, 4, UNIT, 512), column_filter,
        volume.reshape(4, UNIT, 2048), tiles, tile_ray.reshape(1, SLOTS), tile_vox.reshape(1, SLOTS),
    )], live_tiles)
    return new_share.reshape(32, 2048), projected.reshape(2, 512, 1024)


def solution(mesh):
    split = P(("angle", "panel"), None, None)
    return jax.shard_map(
        per_device,
        mesh=mesh,
        in_specs=(
            split, split, P(), P(), P("angle", "panel"), P("panel", None, None), P("panel"), P("panel"), P("panel"),
        ),
        out_specs=(P("angle", "panel"), split),
        check_vma=False,
    )
```

```python
import functools

import jax
import jax.numpy as jnp
from jax import lax
from jax.experimental import pallas as pl
from jax.experimental.pallas import tpu as pltpu
from jax.sharding import PartitionSpec as P

MESH = pl.DeviceIdType.MESH
BF = jnp.bfloat16
F32 = jnp.float32
I32 = jnp.int32
PLANE = 16
NZ = 8
SLOTS = 192
UNROLL = 96
STEP_SIZE = 0.1
UNIT = 8
UNITS = (1, 1, 1, 1)
NC = len(UNITS)
SCHEDULE = (
    "F1 O0 F2 B0", "10 F3 B1 20", "11 U0 B2 21", "12 30 U1 B3", "22 40 13 31", "U2 23 P0 32", "41 U3 P1 42", "33 P2 43 P3",
)
FIRST = tuple(sum(UNITS[:c]) for c in range(NC))


def kernel(
    measured, predicted, sfilt, cfilt, volume, tiles_hbm, ray_hbm, vox_hbm, live_ref,
    new_out, proj_out,
    m_v, p_v, sf_v, cf_v, vol_v, tiles, misfit, across, newvol,
    keys, ray_v, vox_v, idx_v, idx, *rest,
):
    names = (
        "filt", "gath", "slots", "sib_out", "sib_in", "part", "near", "far", "half", "mid", "mid2",
        "vox", "fslots", "stage",
    )
    per_chunk = len(names)
    bufs = [dict(zip(names, rest[c * per_chunk:(c + 1) * per_chunk])) for c in range(NC)]
    (in_sem, idx_sem, a_send, a_recv, sib_send, sib_recv, rs_send, rs_recv,
     ag_send, ag_recv, c_send, c_recv, loc_sem) = rest[NC * per_chunk:]

    a = lax.axis_index("angle")
    pan = lax.axis_index("panel")
    z = pan // 2
    core = pan % 2
    ax, ay = a % 4, a // 4

    def plane_peer(i):
        return ((ay + i // 4) % 4) * 4 + (ax + i) % 4

    def along_z(dz):
        return {"panel": ((z + dz + NZ) % NZ) * 2 + core}

    def units_of(c):
        return pl.ds(FIRST[c], UNITS[c])

    def volume_store(c):
        return pltpu.make_async_copy(newvol.at[units_of(c)], new_out.at[units_of(c)], loc_sem.at[c])

    def own_projection(c):
        return pltpu.make_async_copy(
            bufs[c]["stage"].at[pl.ds(a * 2, 2)], proj_out.at[:, a, units_of(c)], loc_sem.at[NC + c])

    sibling = {"panel": z * 2 + (1 - core)}

    loads = [
        pltpu.make_async_copy(src, dst, in_sem.at[i])
        for i, (src, dst) in enumerate((
            (predicted.at[0], p_v.at[0]), (measured.at[0], m_v.at[0]), (cfilt, cf_v), (sfilt, sf_v),
            (predicted.at[1], p_v.at[1]), (measured.at[1], m_v.at[1]), (tiles_hbm, tiles), (volume, vol_v), (ray_hbm, ray_v), (vox_hbm, vox_v),
        ))
    ]
    for load in loads[:3]:
        load.start()

    barrier = pltpu.get_barrier_semaphore()

    @pl.loop(1, PLANE)
    def _(i):
        pl.semaphore_signal(barrier, inc=1, device_id={"angle": plane_peer(i)}, device_id_type=MESH)

    for peer in (sibling, along_z(1), along_z(-1), along_z(2), along_z(-2)):
        pl.semaphore_signal(barrier, inc=1, device_id=peer, device_id_type=MESH)

    def misfit_rows(k, rows):
        bright = jnp.exp(-p_v[k, rows, :].astype(F32))
        misfit[k, rows, :] = ((m_v[k, rows, :].astype(F32) - bright) * bright).astype(BF)

    def misfit_of(k):
        @pl.loop(0, 4)
        def _(i):
            for u in range(2):
                misfit_rows(k, pl.ds(pl.multiple_of(i * 128 + u * 64, 64), 64))

    def across_of(k, tiles_of_columns, beside=None):
        for n in tiles_of_columns:
            if beside is not None:
                for v in range(4):
                    misfit_rows(beside, pl.ds((n - 2) * 256 + v * 64, 64))
            columns = pl.ds(n * 256, 256)
            across[k, n] = jnp.dot(misfit[k], cf_v[:, columns], preferred_element_type=F32).astype(BF)

    def filter_of(c, k):
        filt = bufs[c]["filt"]
        r = UNITS[c] * UNIT

        rows = sf_v[:, FIRST[c]:FIRST[c] + UNITS[c]].reshape(PLANE * r, 512)
        for n in range(4):
            out = jnp.dot(rows, across[k, n], preferred_element_type=F32).astype(BF)
            for d in range(PLANE):
                for j in range(2):
                    filt[d * 16 + k * 8 + n * 2 + j] = out[d * r:(d + 1) * r, j * 128:(j + 1) * 128]

    def send_filtered(c, at=0, count=16):
        filt, gath = bufs[c]["filt"], bufs[c]["gath"]

        @pl.loop(1, PLANE)
        def _(i):
            peer = plane_peer(i)
            pltpu.make_async_remote_copy(
                src_ref=filt.at[pl.ds(peer * 16 + at, count)],
                dst_ref=gath.at[pl.ds(a * 16 + at, count)],
                send_sem=a_send.at[c], recv_sem=a_recv.at[c],
                device_id={"angle": peer}, device_id_type=MESH,
            ).start()

        gath[pl.ds(a * 16 + at, count)] = filt[pl.ds(a * 16 + at, count)]

    def wait_bytes(ref, sem):
        pltpu.make_async_copy(ref, ref, sem).wait()

    def remote(src, dst, send, recv, device):
        pltpu.make_async_remote_copy(
            src_ref=src, dst_ref=dst, send_sem=send, recv_sem=recv, device_id=device, device_id_type=MESH
        ).start()

    def order_tiles():
        row = lax.broadcasted_iota(I32, (256, 256), 0)
        col = lax.broadcasted_iota(I32, (256, 256), 1)
        dead = 256
        keys[...] = jnp.full((8, 256), dead, I32)
        keys[0:1, 0:SLOTS] = vox_v[...]
        keys[1:2, 0:SLOTS] = ray_v[...]
        live = live_ref[0]

        def down(x):
            return jnp.sum(x, axis=0, keepdims=True)

        def spread(x):
            return jnp.broadcast_to(x, (256, 256))

        def one(main, other, at, address):
            main_row = spread(main)
            main_row = jnp.where(col < live, main_row, dead)
            main_col = main_row.T
            other_col = spread(other).T
            same_before = ((main_col == main_row) & (row < col)).astype(I32)
            before = same_before + (main_col < main_row).astype(I32)
            rank_col = spread(down(before)).T
            repeat_col = spread((down(same_before) > 0).astype(I32)).T
            placed = (rank_col == col).astype(I32)
            idx_v[at:at + 1, :] = down(placed * row)
            idx_v[at + 1:at + 2, :] = address(down(placed * other_col))
            idx_v[at + 2:at + 3, :] = down(placed * repeat_col)
            through = down((main_col <= col).astype(I32)) - 1
            present = down((main_col == col).astype(I32)) > 0
            idx_v[at + 3:at + 4, :] = jnp.where(present, through, SLOTS)

        def voxel_address(v):
            block_z, block_core = (v >> 5) & 7, (v >> 4) & 1
            return block_core * 128 + ((block_z - z + 10) & 7) * 16 + (v & 15)

        one(keys[0:1, :], keys[1:2, :], 0, lambda r: r & 255)
        one(keys[1:2, :], keys[0:1, :], 4, voxel_address)
        move = pltpu.make_async_copy(idx_v, idx, idx_sem)
        move.start()
        move.wait()

    def tile_sums(c, source, slots, at, transposed):
        r = UNITS[c] * UNIT
        blank = jnp.zeros((r, 128), BF)
        slots[SLOTS] = blank
        joined = 0 if transposed else 1
        contract = (((1,), (1,)), ((), ())) if transposed else (((1,), (0,)), ((), ()))

        def four(j, acc):
            ts = [tiles[idx[at, j + i]] for i in range(4)]
            xs = [source[idx[at + 1, j + i]] for i in range(4)]
            left = jnp.concatenate(
                [jnp.concatenate([xs[0], blank], 1), jnp.concatenate([xs[1], blank], 1),
                 jnp.concatenate([blank, xs[2]], 1), jnp.concatenate([blank, xs[3]], 1)], 0)
            right = jnp.concatenate(
                [jnp.concatenate(ts[:2], joined), jnp.concatenate(ts[2:], joined)], 1 - joined)
            out = lax.dot_general(left, right, contract, preferred_element_type=F32)
            for i in range(4):
                lane = (i % 2) * 128
                term = out[i * r:(i + 1) * r, lane:lane + 128]
                acc = acc * idx[at + 2, j + i].astype(F32) + term
                slots[j + i] = acc.astype(BF)
            return acc

        def body(step, acc):
            for u in range(UNROLL // 4):
                acc = four(step * UNROLL + u * 4, acc)
            return acc

        lax.fori_loop(0, SLOTS // UNROLL, body, jnp.zeros((r, 128), F32))

    def panel_block(rel, which):
        return (((z + rel + 6) % NZ) * 2 + which) * 16

    def share(rel):
        return pl.ds(rel * 16, 16)

    def collect_for_sibling(c, first, count):
        b = bufs[c]

        @pl.loop(0, count)
        def _(o):
            base = panel_block(first + o, 1 - core)
            for i in range(16):
                b["sib_out"][(first + o) * 16 + i] = b["slots"][idx[3, base + i]]

    def send_to_sibling(c, part, first, count):
        b = bufs[c]
        where = pl.ds(first * 16, count * 16)
        remote(b["sib_out"].at[where], b["sib_in"].at[where], sib_send.at[c], sib_recv.at[c, part], sibling)

    def back_project(c):
        b = bufs[c]
        wait_bytes(b["gath"].at[pl.ds(0, 240)], a_recv.at[c])
        tile_sums(c, b["gath"], b["slots"], 0, False)
        collect_for_sibling(c, 5, 3)
        send_to_sibling(c, 0, 5, 3)
        collect_for_sibling(c, 0, 5)
        send_to_sibling(c, 1, 0, 5)

    def wait_sibling(c, part, first, count):
        where = pl.ds(first * 16, count * 16)
        wait_bytes(bufs[c]["sib_in"].at[where], sib_recv.at[c, part])

    def pair_sum(c, rel, i):
        b = bufs[c]
        own = b["slots"][idx[3, panel_block(rel, core) + i]]
        return own.astype(F32) + b["sib_in"][rel * 16 + i].astype(F32)

    def make_part(c, rel):
        part = bufs[c]["part"]
        for i in range(16):
            part[rel * 16 + i] = pair_sum(c, rel, i).astype(BF)

    def reduce_first(c):
        b = bufs[c]
        wait_sibling(c, 0, 5, 3)
        for rel in (5, 7, 6):
            make_part(c, rel)
        for way, sign, far_rel in ((0, 1, 5), (1, -1, 7)):
            remote(b["part"].at[share(far_rel)], b["far"].at[way], rs_send.at[c], rs_recv.at[c, way], along_z(sign))
            half = pl.ds(6 * 16 + way * 8, 8)
            remote(b["part"].at[half], b["half"].at[way], rs_send.at[c], rs_recv.at[c, 2 + way], along_z(2 * sign))
        wait_sibling(c, 1, 0, 5)
        for way, sign, rel in ((0, 1, 3), (1, -1, 1)):
            make_part(c, rel)
            remote(b["part"].at[share(rel)], b["near"].at[way], rs_send.at[c], rs_recv.at[c, 4 + way], along_z(sign))

    def reduce_second(c):
        b = bufs[c]
        for way, sign, rel in ((0, 1, 4), (1, -1, 0)):
            wait_bytes(b["far"].at[way], rs_recv.at[c, way])
            wait_bytes(b["half"].at[way], rs_recv.at[c, 2 + way])
            for i in range(16):
                total = pair_sum(c, rel, i) + b["far"][way, i].astype(F32)
                if i // 8 == way:
                    total = total + b["half"][way, i % 8].astype(F32)
                b["mid"][way, i] = total.astype(BF)
            remote(b["mid"].at[way], b["mid2"].at[way], rs_send.at[c], rs_recv.at[c, 6 + way], along_z(2 * sign))

    def update(c):
        b = bufs[c]
        for way in range(2):
            wait_bytes(b["near"].at[way], rs_recv.at[c, 4 + way])
            wait_bytes(b["mid2"].at[way], rs_recv.at[c, 6 + way])
        mine = core * 128 + 2 * 16
        for i in range(16):
            total = pair_sum(c, 2, i)
            for way in range(2):
                total = total + b["near"][way, i].astype(F32) + b["mid2"][way, i].astype(F32)
            lanes = slice(i * 128, (i + 1) * 128)
            old = vol_v[units_of(c), :, lanes].reshape(UNITS[c] * UNIT, 128)
            new = jnp.clip(old + STEP_SIZE * total, 0.0, 1.0)
            newvol[units_of(c), :, lanes] = new.reshape(UNITS[c], UNIT, 128)
            b["vox"][mine + i] = new.astype(BF)
        base = core * 128
        own = b["vox"].at[pl.ds(mine, 16)]
        for n, (dz, rel) in enumerate(((2, 0), (-2, 4), (1, 1), (-1, 3))):
            remote(own, b["vox"].at[pl.ds(base + rel * 16, 16)], ag_send.at[c], ag_recv.at[c, n], along_z(dz))
        volume_store(c).start()

    def gather_second(c):
        b = bufs[c]
        base = core * 128
        vox = b["vox"]
        for way, sign, came, goes in ((0, 1, 0, 7), (1, -1, 4, 5)):
            block = vox.at[pl.ds(base + came * 16, 16)]
            wait_bytes(block, ag_recv.at[c, way])
            remote(block, vox.at[pl.ds(base + goes * 16, 16)], ag_send.at[c], ag_recv.at[c, 4 + way], along_z(sign))
            remote(
                vox.at[pl.ds(base + came * 16 + way * 8, 8)], vox.at[pl.ds(base + 6 * 16 + way * 8, 8)],
                ag_send.at[c], ag_recv.at[c, 6 + way], along_z(2 * sign))
        for n, rel in ((2, 1), (3, 3)):
            wait_bytes(vox.at[pl.ds(base + rel * 16, 16)], ag_recv.at[c, n])
        first = vox.at[pl.ds(base, 80)]
        remote(first, first, ag_send.at[c], sib_recv.at[c, 2], sibling)

    def gather_third(c):
        vox = bufs[c]["vox"]
        base = core * 128
        for way, goes in ((0, 7), (1, 5)):
            wait_bytes(vox.at[pl.ds(base + goes * 16, 16)], ag_recv.at[c, 4 + way])
            wait_bytes(vox.at[pl.ds(base + 6 * 16 + way * 8, 8)], ag_recv.at[c, 6 + way])
        last = vox.at[pl.ds(base + 80, 48)]
        remote(last, last, ag_send.at[c], sib_recv.at[c, 3], sibling)

    def project(c):
        b = bufs[c]
        vox, stage, fslots = b["vox"], b["stage"], b["fslots"]
        other = (1 - core) * 128
        wait_bytes(vox.at[pl.ds(other, 80)], sib_recv.at[c, 2])
        wait_bytes(vox.at[pl.ds(other + 80, 48)], sib_recv.at[c, 3])
        tile_sums(c, vox, fslots, 4, True)

        @pl.loop(0, 32)
        def _(k):
            for j in range(8):
                block = fslots[idx[7, k * 8 + j]]
                stage[k, :, :, j * 128:(j + 1) * 128] = block.reshape(UNITS[c], UNIT, 128)

        @pl.loop(1, PLANE)
        def _(i):
            peer = plane_peer(i)
            remote(stage.at[pl.ds(peer * 2, 2)], proj_out.at[:, a, units_of(c)], c_send.at[c], c_recv.at[c], {"angle": peer})

        own_projection(c).start()

    for load in loads[:2]:
        load.wait()
    for load in loads[3:6]:
        load.start()
    misfit_of(0)
    loads[2].wait()
    across_of(0, (0, 1))
    for load in loads[3:6]:
        load.wait()
    for load in loads[6:]:
        load.start()
    across_of(0, (2, 3), 1)
    filter_of(0, 0)
    pl.semaphore_wait(barrier, PLANE - 1 + 5)
    send_filtered(0, 0, 8)
    across_of(1, range(4))
    filter_of(0, 1)
    send_filtered(0, 8, 8)

    def filter_chunk(c):
        for k in range(2):
            filter_of(c, k)
        send_filtered(c)

    def order_step(_):
        for load in loads[8:]:
            load.wait()
        order_tiles()
        for load in loads[6:8]:
            load.wait()

    stages = {
        "B": back_project, "1": reduce_first, "2": reduce_second, "U": update, "3": gather_second,
        "4": gather_third, "P": project, "F": filter_chunk, "O": order_step,
    }
    for step in " ".join(SCHEDULE).split():
        stages[step[0]](int(step[1]))

    for c in range(NC):
        b = bufs[c]
        wait_bytes(b["filt"].at[pl.ds(0, 240)], a_send.at[c])
        wait_bytes(b["sib_out"], sib_send.at[c])
        wait_bytes(b["vox"].at[pl.ds(0, 112)], rs_send.at[c])
        wait_bytes(b["vox"].at[pl.ds(0, 112 + 128)], ag_send.at[c])
        volume_store(c).wait()
        own_projection(c).wait()
        wait_bytes(b["stage"].at[pl.ds(0, 30)], c_send.at[c])
        wait_bytes(b["stage"].at[pl.ds(0, 30)], c_recv.at[c])


def store_kernel(share, projected, share_out, projected_out, sem):
    copies = []
    for i in range(8):
        at = i // 4, pl.ds((i % 4) * 128, 128)
        copies.append(pltpu.make_async_copy(projected.at[at], projected_out.at[at], sem.at[i]))
    copies.append(pltpu.make_async_copy(share, share_out, sem.at[8]))
    for copy in copies:
        copy.start()
    for copy in copies:
        copy.wait()


def stored(share, projected):
    return pl.pallas_call(
        store_kernel,
        out_shape=(
            jax.ShapeDtypeStruct(share.shape, share.dtype), jax.ShapeDtypeStruct(projected.shape, projected.dtype)),
        in_specs=[pl.BlockSpec(memory_space=pl.ANY)] * 2,
        out_specs=(pl.BlockSpec(memory_space=pltpu.HBM), pl.BlockSpec(memory_space=pltpu.HBM)),
        scratch_shapes=[pltpu.SemaphoreType.DMA((9,))],
        name="store_results",
    )(*[pltpu.with_memory_space_constraint(x, pltpu.VMEM) for x in (share, projected)])


def per_device(measured, predicted, slice_filter, column_filter, volume, tiles, tile_ray, tile_vox, live_tiles):
    V = pltpu.VMEM
    D = pltpu.SemaphoreType.DMA
    chunks = []
    for u in UNITS:
        r = u * UNIT
        share = (16, r, 128)
        chunks += [
            V((256, r, 128), BF),
            V((256, r, 128), BF),
            V((SLOTS + 1, r, 128), BF),
            V((128, r, 128), BF),
            V((128, r, 128), BF),
            V((128, r, 128), BF),
            V((2,) + share, BF),
            V((2,) + share, BF),
            V((2, 8, r, 128), BF),
            V((2,) + share, BF),
            V((2,) + share, BF),
            V((256, r, 128), BF),
            V((SLOTS + 1, r, 128), BF),
            V((32, u, UNIT, 1024), BF),
        ]
    scratch = [
        V((2, 512, 1024), BF), V((2, 512, 1024), BF), V((PLANE, 4, UNIT, 512), BF), V((1024, 1024), BF),
        V((4, UNIT, 2048), F32), V((SLOTS, 128, 128), BF), V((2, 512, 1024), BF), V((2, 4, 512, 256), BF),
        V((4, UNIT, 2048), F32), V((8, 256), I32), V((1, SLOTS), I32), V((1, SLOTS), I32), V((8, 256), I32), pltpu.SMEM((8, 256), I32),
    ] + chunks + [
        D((10,)), D, D((NC,)), D((NC,)), D((NC,)), D((NC, 4)), D((NC,)), D((NC, 8)),
        D((NC,)), D((NC, 8)), D((NC,)), D((NC,)), D((2 * NC,)),
    ]
    anywhere = pl.BlockSpec(memory_space=pl.ANY)
    new_share, projected = pl.pallas_call(
        kernel,
        out_shape=(
            jax.ShapeDtypeStruct((4, UNIT, 2048), F32),
            jax.ShapeDtypeStruct((2, PLANE, 4, UNIT, 1024), BF),
        ),
        in_specs=[pl.BlockSpec(memory_space=pltpu.HBM)] * 8 + [pl.BlockSpec(memory_space=pltpu.SMEM)],
        out_specs=(anywhere, anywhere),
        scratch_shapes=scratch,
        compiler_params=pltpu.CompilerParams(
            collective_id=0, has_side_effects=True, vmem_limit_bytes=36 * 1024 * 1024
        ),
        name="tomography_iteration",
    )(*[pltpu.with_memory_space_constraint(x, pltpu.HBM) for x in (
        measured, predicted, slice_filter.reshape(PLANE, 4, UNIT, 512), column_filter,
        volume.reshape(4, UNIT, 2048), tiles, tile_ray.reshape(1, SLOTS), tile_vox.reshape(1, SLOTS),
    )], live_tiles)
    return stored(new_share.reshape(32, 2048), projected.reshape(2, 512, 1024))


def solution(mesh):
    split = P(("angle", "panel"), None, None)
    return jax.shard_map(
        per_device,
        mesh=mesh,
        in_specs=(
            split, split, P(), P(), P("angle", "panel"), P("panel", None, None), P("panel"), P("panel"), P("panel"),
        ),
        out_specs=(P("angle", "panel"), split),
        check_vma=False,
    )
```
